128 devices in a mesh: row: 16 (over z_hi, y, core), col: 8 (over x, z_lo).
Axes of the slice: x: 4, y: 4, z: 4 (z_hi: 2, z_lo: 2; z = z_hi * 2 + z_lo), core: 2. Of those that a mesh axis runs over, the one named last changes fastest.
Arguments:
- embeddings: bfloat16 [65536, 2560], P(('row', 'col')), may hold values from -6 to 6
- weight_in: bfloat16 [2560, 1024], replicated, may hold values from -0.125 to 0.125
- bias_in: float32 [1024], replicated, may hold values from -3 to 3
- weight_out: bfloat16 [1024, 64], replicated, may hold values from -0.1875 to 0.1875
- lengthscale: float32 [1], replicated, may hold values from 2 to 2.64
- noise_level: float32 [1], replicated, may hold values from 0.3 to 1
- right_side: float32 [33, 65536], P(None, ('row', 'col')), may hold values from -51 to 51
Outputs:
- residual: float32 [33, 65536], P(None, ('row', 'col'))
- direction: float32 [33, 65536], P(None, ('row', 'col'))
- step_size: float32 [33], replicated
- correction: float32 [33], replicated
The draws below stay inside these ranges and needn't reach their ends.
All inputs are finite; a program needn't handle non-finite values.
Results may differ from the reference program's by a relative error of at most 0.0055.
Values may be sent and summed in bfloat16 or wider, within the bound.
A program may use at most 128 MiB of HBM per device.

```python
import math
import jax
import jax.numpy as jnp
from jax import lax

EMBED = 2560
INNER = 1024
FEAT = 64
COLS = 33
TOTAL = 65536


def draw_right_side(key, part):
    key = jax.random.fold_in(key, 11)
    keys = jax.random.split(key, 3)
    col_scale = jnp.exp(jax.random.uniform(keys[0], (COLS, 1), jnp.float32, math.log(0.3), math.log(3.0)))
    position = jnp.arange(TOTAL, dtype=jnp.float32) / TOTAL
    rising = jnp.exp(math.log(3.0) * position)[None, :]
    rough = jnp.exp(jax.random.uniform(keys[1], (1, TOTAL), jnp.float32, math.log(0.6), math.log(1.4)))
    base = jnp.clip(jax.random.normal(keys[2], (COLS, TOTAL), jnp.float32), -4.0, 4.0)
    return (base * col_scale * rising * rough).astype(jnp.float32)


def level_of(key, dims, cuts, smallest, largest):
    def one(axis_at, parts):
        heights = jax.random.uniform(jax.random.fold_in(jax.random.fold_in(key, 6), axis_at), (parts,), jnp.float32, smallest / len(cuts), largest / len(cuts))
        return jnp.repeat(jnp.exp(heights), dims[axis_at] // parts).reshape((-1,) + (1,) * (len(dims) - axis_at - 1))

    loudness = one(*cuts[0])
    for cut in cuts[1:]:
        loudness = loudness * one(*cut)
    return loudness


def centred(own_key, dims, width, bound, cuts=(), kind=jnp.bfloat16):
    gain = level_of(own_key, dims, cuts, -0.22, 0.18) if cuts else 1.0
    values = jax.random.normal(own_key, dims, jnp.float32) * width * gain
    return jnp.minimum(jnp.maximum(values, -bound), bound).astype(kind)


def setup_inputs(seed: int = 0) -> dict:
    seeds = jax.random.split(jax.random.key(seed), 8)
    return {
        "embeddings": centred(seeds[0], (TOTAL, EMBED), 1.0, 6.0, ((0, 128),)),
        "weight_in": centred(seeds[1], (EMBED, INNER), EMBED ** -0.5, 0.125),
        "bias_in": centred(seeds[2], (INNER,), 0.5, 3.0, (), jnp.float32),
        "weight_out": centred(seeds[3], (INNER, FEAT), INNER ** -0.5, 0.1875),
        "lengthscale": jnp.clip(jnp.exp(jax.random.uniform(seeds[4], (1,), jnp.float32, math.log(2.0), math.log(2.64))), 2.0, 2.64),
        "noise_level": jnp.clip(jnp.exp(jax.random.uniform(seeds[5], (1,), jnp.float32, math.log(0.3), math.log(1.0))), 0.3, 1.0),
        "right_side": draw_right_side(jax.random.fold_in(seeds[7], 71), 0),
    }


def reference(embeddings, weight_in, bias_in, weight_out, lengthscale, noise_level, right_side):
    hidden = jax.nn.gelu(jnp.dot(embeddings, weight_in, preferred_element_type=jnp.float32) + bias_in, approximate=False).astype(jnp.bfloat16)
    features = jnp.dot(hidden, weight_out, preferred_element_type=jnp.float32).astype(jnp.bfloat16)
    feat_wide = features.astype(jnp.float32)
    squares = jnp.sum(feat_wide * feat_wide, axis=1)
    exponent_scale = 0.5 / (lengthscale[0] * lengthscale[0])
    probe_half = right_side.astype(jnp.bfloat16)
    block_size = math.gcd(1024, TOTAL)
    block_count = TOTAL // block_size

    def tile_block(block_index):
        start = (block_index * block_size).astype(jnp.int32)
        rows_feat = lax.dynamic_slice_in_dim(features, start, block_size, 0)
        rows_norm = lax.dynamic_slice_in_dim(squares, start, block_size, 0)
        inner = lax.dot_general(rows_feat, features, (((1,), (1,)), ((), ())), preferred_element_type=jnp.float32)
        distance = rows_norm[:, None] + squares[None, :] - 2.0 * inner
        kernel = jnp.exp(-distance * exponent_scale).astype(jnp.bfloat16)
        return lax.dot_general(probe_half, kernel, (((1,), (1,)), ((), ())), preferred_element_type=jnp.float32)

    pieces = lax.map(tile_block, jnp.arange(block_count, dtype=jnp.int32))
    products = jnp.transpose(pieces, (1, 0, 2)).reshape(COLS, TOTAL)
    images = products + noise_level[0] * right_side
    norm_old = jnp.sum(right_side * right_side, axis=1)
    curvature = jnp.sum(right_side * images, axis=1)
    step_size = norm_old / curvature
    residual = right_side - step_size[:, None] * images
    norm_new = jnp.sum(residual * residual, axis=1)
    correction = norm_new / norm_old
    direction = residual + correction[:, None] * right_side
    return residual, direction, step_size, correction
```

```python
import functools
import math

import jax
import jax.numpy as jnp
from jax import lax
from jax.experimental import pallas as pl
from jax.experimental.pallas import tpu as pltpu
from jax.sharding import PartitionSpec as P

MESH = pl.DeviceIdType.MESH
F32 = jnp.float32
BF16 = jnp.bfloat16

LINES = 16
MEMBERS = 8
BLOCK = 512
HALF = 256
SPAN = MEMBERS * HALF
FEAT = 64
EMBED = 2560
INNER = 1024
COLS = 33
PROBE_ROWS = 48
SUM_ROWS = 40
STRIP = 1024
SUB = 512
NCHUNK = 256


def device_of(line, member):
    y, z = line // 4, line % 4
    x, core = member // 2, member % 2
    return ((z // 2) * 8 + y * 2 + core, x * 2 + z % 2)


def gelu(v):
    return 0.5 * v * (1.0 + lax.erf(v * (1.0 / math.sqrt(2.0))))


def pieces_of(v):
    first = v.astype(BF16).astype(F32)
    rest = v - first
    second = rest.astype(BF16).astype(F32)
    third = (rest - second).astype(BF16).astype(F32)
    return first, second, third


def kernel(
    emb, w_in, bias, w_out, scale_in, noise_in, rs_in,
    img_out, sc_out,
    x_buf, w_buf, b_buf, wo_buf, rs_buf, rs_pad, p_own, probes, feats, at, bb,
    acc_a, acc_b, parts, stat_own, stat_line, stat_mid, stat_all,
    load_sem, ps_sem, pr_sem, fs_sem, fr_sem, qs_sem, qr_sem, s1_sem, r1_sem, s2_sem, r2_sem,
):
    row, col = lax.axis_index("row"), lax.axis_index("col")
    line = ((row // 2) % 4) * 4 + (row // 8) * 2 + col % 2
    member = (col // 2) * 2 + row % 2
    b_line = (line + member + 1) % LINES

    def mate(j):
        return (member + j) % MEMBERS

    def target(k):
        return device_of((line + LINES - k) % LINES, k - 1)

    loads = []

    def load(src, dst):
        c = pltpu.make_async_copy(src, dst, load_sem.at[len(loads)])
        c.start()
        loads.append(c)
        return c

    load_rs = load(rs_in, rs_buf)
    load_x = [load(emb.at[pl.ds(0, HALF), :], x_buf.at[0])]
    load_w = [
        load(w_in.at[:, pl.ds(n * NCHUNK, NCHUNK)], w_buf.at[n]) for n in range(INNER // NCHUNK)
    ]
    load_b = load(bias, b_buf)
    load_wo = load(w_out, wo_buf)
    load_x.append(load(emb.at[pl.ds(HALF, HALF), :], x_buf.at[1]))

    barrier = pltpu.get_barrier_semaphore()

    def greet(device):
        pl.semaphore_signal(barrier, inc=1, device_id=device, device_id_type=MESH)

    @pl.loop(1, MEMBERS)
    def _(j):
        greet(device_of(line, mate(j)))

    @pl.loop(0, MEMBERS)
    def _(j):
        greet(target(j + 1))
        greet(device_of(b_line, j))

    @pl.loop(1, LINES)
    def _(j):
        greet(device_of((line + j) % LINES, member))

    load_rs.wait()
    rs_pad[...] = jnp.zeros_like(rs_pad)
    rs_pad[pl.ds(0, COLS), :] = rs_buf[...]
    for h in range(2):
        p_own[h] = rs_pad[:, pl.ds(h * HALF, HALF)].astype(BF16)
    own = pl.ds(pl.multiple_of(member * HALF, HALF), HALF)
    for h in range(2):
        probes[2 + h, :, own] = p_own[h]

    acc_a[...] = jnp.zeros_like(acc_a)
    acc_b[...] = jnp.zeros_like(acc_b)

    pl.semaphore_wait(barrier, 7 + 8 + 8 + 15)

    def probe_copy(base, sem_at, recv_at, device):
        return pltpu.make_async_remote_copy(
            src_ref=p_own,
            dst_ref=probes.at[pl.ds(base, 2), :, own],
            send_sem=ps_sem.at[sem_at],
            recv_sem=pr_sem.at[recv_at],
            device_id=device,
            device_id_type=MESH,
        )

    @pl.loop(1, MEMBERS)
    def _(j):
        probe_copy(2, j, member, device_of(line, mate(j))).start()

    @pl.loop(0, MEMBERS)
    def _(j):
        probe_copy(0, MEMBERS + j, MEMBERS + member, target(j + 1)).start()

    def feat_copy(h, base, sem_at, recv_at, device):
        return pltpu.make_async_remote_copy(
            src_ref=feats.at[2 + h, :, own],
            dst_ref=feats.at[base + h, :, own],
            send_sem=fs_sem.at[h, sem_at],
            recv_sem=fr_sem.at[h, recv_at],
            device_id=device,
            device_id_type=MESH,
        )

    for h in range(2):
        load_x[h].wait()
        total = jnp.zeros((HALF, FEAT), F32)
        for n in range(INNER // NCHUNK):
            if h == 0:
                load_w[n].wait()
                if n == 0:
                    load_b.wait()
                    load_wo.wait()
            pre = jnp.dot(x_buf[h], w_buf[n], preferred_element_type=F32)
            hidden = gelu(pre + b_buf[:, pl.ds(n * NCHUNK, NCHUNK)]).astype(BF16)
            total += jnp.dot(
                hidden, wo_buf[pl.ds(n * NCHUNK, NCHUNK), :], preferred_element_type=F32
            )
        feats[2 + h, :, own] = total.T.astype(BF16)

        @pl.loop(1, MEMBERS)
        def _(j):
            feat_copy(h, 2, j, member, device_of(line, mate(j))).start()

        @pl.loop(0, MEMBERS)
        def _(j):
            feat_copy(h, 0, MEMBERS + j, MEMBERS + member, target(j + 1)).start()

    length = jnp.full((1, SPAN), scale_in[0], F32)
    unit = (1.0 / math.log(2.0)) / (length * length)
    level = lax.broadcasted_iota(jnp.int32, (FEAT, SPAN), 0)

    def extras(norm, at_norm, at_one):
        one, two, three = pieces_of(norm)
        out = jnp.where((level >= at_one) & (level < at_one + 3), 1.0, 0.0)
        for i, piece in enumerate((one, two, three)):
            out = jnp.where(level == at_norm + i, jnp.broadcast_to(piece, out.shape), out)
        return out

    def build_columns(half):
        wide = feats[half].astype(F32)
        norm = jnp.sum(wide * wide, axis=0, keepdims=True) * (unit * -0.5)
        for i, piece in enumerate(pieces_of(wide * unit)):
            bb[half, pl.ds(i * FEAT, FEAT), :] = piece.astype(BF16)
        bb[half, pl.ds(3 * FEAT, FEAT), :] = extras(norm, 0, 3).astype(BF16)

    def build_rows(h):
        wide = feats[2 + h].astype(F32)
        norm = jnp.sum(wide * wide, axis=0, keepdims=True) * (unit * -0.5)
        at[h, :, pl.ds(0, 128)] = jnp.concatenate([wide, wide], axis=0).T.astype(BF16)
        at[h, :, pl.ds(128, 128)] = jnp.concatenate([wide, extras(norm, 3, 0)], axis=0).T.astype(BF16)

    def wait_half(h):
        @pl.loop(1, MEMBERS)
        def _(j):
            feat_copy(h, 2, j, mate(j), device_of(line, mate(j))).wait_recv()

        @pl.loop(0, MEMBERS)
        def _(j):
            feat_copy(h, 0, j, MEMBERS + j, device_of(b_line, j)).wait_recv()

    def strip(a, b, at_col, both):
        cols = bb[b, :, pl.ds(at_col, STRIP)]
        down = jnp.zeros((PROBE_ROWS, STRIP), F32)
        for i in range(SPAN // SUB):
            rows = pl.ds(i * SUB, SUB)
            power = jnp.dot(at[a, rows, :], cols, preferred_element_type=F32)
            tile = jnp.exp2(power).astype(BF16)
            down += jnp.dot(probes[2 + a, :, rows], tile, preferred_element_type=F32)
            if both:
                acc_a[a, :, rows] += lax.dot_general(
                    probes[b, :, pl.ds(at_col, STRIP)], tile, (((1,), (1,)), ((), ())),
                    preferred_element_type=F32,
                )
        acc_b[b, :, pl.ds(at_col, STRIP)] += down

    def quad(a, b, both):
        @pl.loop(0, SPAN // STRIP)
        def _(i):
            strip(a, b, pl.multiple_of(i * STRIP, STRIP), both)

    @pl.loop(1, MEMBERS)
    def _(j):
        probe_copy(2, j, mate(j), device_of(line, mate(j))).wait_recv()

    @pl.loop(0, MEMBERS)
    def _(j):
        probe_copy(0, j, MEMBERS + j, device_of(b_line, j)).wait_recv()

    wait_half(0)
    build_rows(0)
    build_columns(0)

    @pl.when(member < 7)
    def _():
        quad(0, 0, True)

    @pl.when(member == 7)
    def _():
        build_columns(2)
        quad(0, 2, False)

    wait_half(1)
    build_rows(1)
    build_columns(1)

    @pl.when(member == 7)
    def _():
        build_columns(3)
        quad(1, 3, False)

    last = member // 7
    w = line // 8

    @pl.loop(0, 3)
    def _(t):
        second, third = t % 2, t // 2
        is_first = (2 - t) // 2
        a_pair = 1 - is_first
        b_pair = 1 - third
        a_last = second
        b_last = is_first * w + second * (1 - w) + third * 3
        quad(a_pair * (1 - last) + a_last * last, b_pair * (1 - last) + b_last * last, True)

    @pl.when(member == 7)
    def _():
        for h in range(2):
            acc_a[h] += acc_b[2 + h]

    def part_copy(kind, block, sem_at, recv_at, device):
        src = (acc_a, acc_b)[kind]
        return pltpu.make_async_remote_copy(
            src_ref=src.at[
                pl.ds(0, 2), pl.ds(0, SUM_ROWS), pl.ds(pl.multiple_of(block * HALF, HALF), HALF)
            ],
            dst_ref=parts.at[recv_at],
            send_sem=qs_sem.at[sem_at],
            recv_sem=qr_sem.at[recv_at],
            device_id=device,
            device_id_type=MESH,
        )

    @pl.loop(0, MEMBERS)
    def _(j):
        part_copy(1, j, MEMBERS + j, MEMBERS + member, device_of(b_line, j)).start()

    @pl.loop(1, MEMBERS)
    def _(j):
        part_copy(0, mate(j), j, member, device_of(line, mate(j))).start()

    images = [
        acc_a[h, pl.ds(0, SUM_ROWS), own]
        + noise_in[0] * rs_pad[pl.ds(0, SUM_ROWS), pl.ds(h * HALF, HALF)]
        for h in range(2)
    ]

    @pl.loop(1, MEMBERS)
    def _(j):
        part_copy(0, mate(j), j, mate(j), device_of(line, mate(j))).wait_recv()

    @pl.loop(0, MEMBERS)
    def _(j):
        part_copy(1, j, j, MEMBERS + j, target(j + 1)).wait_recv()

    parts[member] = jnp.zeros((2, SUM_ROWS, HALF), F32)
    for h in range(2):
        images[h] = images[h] + jnp.sum(parts[:, h], axis=0)
        img_out[:, pl.ds(h * HALF, HALF)] = images[h][:COLS]

    right = [rs_pad[pl.ds(0, SUM_ROWS), pl.ds(h * HALF, HALF)] for h in range(2)]

    def over(terms):
        return sum(jnp.sum(t, axis=1, keepdims=True) for t in terms)

    def ratio(top, bottom):
        return jnp.where(bottom > 0.0, top / jnp.where(bottom > 0.0, bottom, 1.0), 0.0)

    norm = over([r * r for r in right])
    curve = over([r * i for r, i in zip(right, images)])
    alpha = ratio(curve, norm)
    spread = over([(i - alpha * r) * (i - alpha * r) for r, i in zip(right, images)])
    lane = lax.broadcasted_iota(jnp.int32, (SUM_ROWS, 128), 1)

    def packed(values):
        out = jnp.zeros((SUM_ROWS, 128), F32)
        for i, v in enumerate(values):
            out = jnp.where(lane == i, jnp.broadcast_to(v, out.shape), out)
        return out

    def merged(stats):
        norms, curves, spreads = (stats[:, :, i : i + 1] for i in range(3))
        norm = jnp.sum(norms, axis=0)
        curve = jnp.sum(curves, axis=0)
        shift = ratio(curves, norms) - ratio(curve, norm)[None]
        return norm, curve, jnp.sum(spreads + norms * shift * shift, axis=0)

    stat_own[...] = packed((norm, curve, spread))

    def line_copy(sem_at, recv_at, device):
        return pltpu.make_async_remote_copy(
            src_ref=stat_own, dst_ref=stat_line.at[recv_at],
            send_sem=s1_sem.at[sem_at], recv_sem=r1_sem.at[recv_at],
            device_id=device, device_id_type=MESH,
        )

    @pl.loop(1, MEMBERS)
    def _(j):
        line_copy(j, member, device_of(line, mate(j))).start()

    @pl.loop(1, MEMBERS)
    def _(j):
        line_copy(j, mate(j), device_of(line, mate(j))).wait_recv()

    stat_line[member] = stat_own[...]
    stat_mid[...] = packed(merged(stat_line[...]))

    def across(j):
        return (line + j) % LINES

    def all_copy(sem_at, recv_at, device):
        return pltpu.make_async_remote_copy(
            src_ref=stat_mid, dst_ref=stat_all.at[recv_at],
            send_sem=s2_sem.at[sem_at], recv_sem=r2_sem.at[recv_at],
            device_id=device, device_id_type=MESH,
        )

    @pl.loop(1, LINES)
    def _(j):
        all_copy(j, line, device_of(across(j), member)).start()

    @pl.loop(1, LINES)
    def _(j):
        all_copy(j, across(j), device_of(across(j), member)).wait_recv()

    stat_all[line] = stat_mid[...]
    norm, curve, spread = merged(stat_all[...])
    step = norm / curve
    sc_out[...] = packed((step, step * step * spread / norm))[:COLS]

    @pl.loop(1, MEMBERS)
    def _(j):
        there = device_of(line, mate(j))
        probe_copy(2, j, member, there).wait_send()
        feat_copy(0, 2, j, member, there).wait_send()
        feat_copy(1, 2, j, member, there).wait_send()
        part_copy(0, mate(j), j, member, there).wait_send()
        line_copy(j, member, there).wait_send()

    @pl.loop(0, MEMBERS)
    def _(j):
        there = target(j + 1)
        probe_copy(0, MEMBERS + j, MEMBERS + member, there).wait_send()
        feat_copy(0, 0, MEMBERS + j, MEMBERS + member, there).wait_send()
        feat_copy(1, 0, MEMBERS + j, MEMBERS + member, there).wait_send()
        part_copy(1, j, MEMBERS + j, MEMBERS + member, device_of(b_line, j)).wait_send()

    @pl.loop(1, LINES)
    def _(j):
        all_copy(j, line, device_of(across(j), member)).wait_send()


def on_device(embeddings, weight_in, bias_in, weight_out, lengthscale, noise_level, right_side):
    anywhere = pl.BlockSpec(memory_space=pl.ANY)
    scalar = pl.BlockSpec(memory_space=pltpu.SMEM)
    vmem = pl.BlockSpec(memory_space=pltpu.VMEM)
    dma = pltpu.SemaphoreType.DMA
    images, scalars = pl.pallas_call(
        kernel,
        out_shape=(
            jax.ShapeDtypeStruct((COLS, BLOCK), F32),
            jax.ShapeDtypeStruct((COLS, 128), F32),
        ),
        in_specs=[anywhere, anywhere, anywhere, anywhere, scalar, scalar, anywhere],
        out_specs=[vmem, vmem],
        scratch_shapes=[
            pltpu.VMEM((2, HALF, EMBED), BF16),
            pltpu.VMEM((INNER // NCHUNK, EMBED, NCHUNK), BF16),
            pltpu.VMEM((1, INNER), F32),
            pltpu.VMEM((INNER, FEAT), BF16),
            pltpu.VMEM((COLS, BLOCK), F32),
            pltpu.VMEM((PROBE_ROWS, BLOCK), F32),
            pltpu.VMEM((2, PROBE_ROWS, HALF), BF16),
            pltpu.VMEM((4, PROBE_ROWS, SPAN), BF16),
            pltpu.VMEM((4, FEAT, SPAN), BF16),
            pltpu.VMEM((2, SPAN, 256), BF16),
            pltpu.VMEM((4, 256, SPAN), BF16),
            pltpu.VMEM((2, PROBE_ROWS, SPAN), F32),
            pltpu.VMEM((4, PROBE_ROWS, SPAN), F32),
            pltpu.VMEM((2 * MEMBERS, 2, SUM_ROWS, HALF), F32),
            pltpu.VMEM((SUM_ROWS, 128), F32),
            pltpu.VMEM((MEMBERS, SUM_ROWS, 128), F32),
            pltpu.VMEM((SUM_ROWS, 128), F32),
            pltpu.VMEM((LINES, SUM_ROWS, 128), F32),
            dma((9,)),
            dma((2 * MEMBERS,)),
            dma((2 * MEMBERS,)),
            dma((2, 2 * MEMBERS)),
            dma((2, 2 * MEMBERS)),
            dma((2 * MEMBERS,)),
            dma((2 * MEMBERS,)),
            dma((MEMBERS,)),
            dma((MEMBERS,)),
            dma((LINES,)),
            dma((LINES,)),
        ],
        compiler_params=pltpu.CompilerParams(
            collective_id=0, has_side_effects=True, vmem_limit_bytes=56 * 2**20
        ),
        name="cg_step",
    )(
        embeddings, weight_in, bias_in.reshape(1, INNER), weight_out, lengthscale, noise_level,
        right_side,
    )
    step_size = scalars[:, 0]
    correction = scalars[:, 1]
    residual = right_side - step_size[:, None] * images
    direction = residual + correction[:, None] * right_side
    return (residual, direction, step_size, correction)


def solution(mesh):
    in_specs = (P(("row", "col"), None), P(), P(), P(), P(), P(), P(None, ("row", "col")))
    out_specs = (P(None, ("row", "col")), P(None, ("row", "col")), P(), P())
    return jax.shard_map(
        on_device, mesh=mesh, in_specs=in_specs, out_specs=out_specs, check_vma=False
    )
```

```python
import functools
import math

import jax
import jax.numpy as jnp
from jax import lax
from jax.experimental import pallas as pl
from jax.experimental.pallas import tpu as pltpu
from jax.sharding import PartitionSpec as P

MESH = pl.DeviceIdType.MESH
F32 = jnp.float32
BF16 = jnp.bfloat16

LINES = 16
MEMBERS = 8
BLOCK = 512
HALF = 256
SPAN = MEMBERS * HALF
FEAT = 64
GATHERED = FEAT + 48
EMBED = 2560
INNER = 1024
COLS = 33
PROBE_ROWS = 48
SUM_ROWS = 40
PIECE = 1024
SUB = 512
NCHUNK = 256


def device_of(x, y, z, core):
    return ((z // 2) * 8 + y * 2 + core, x * 2 + z % 2)


def gelu(v):
    return 0.5 * v * (1.0 + lax.erf(v * (1.0 / math.sqrt(2.0))))


def pieces_of(v):
    first = v.astype(BF16).astype(F32)
    rest = v - first
    second = rest.astype(BF16).astype(F32)
    third = (rest - second).astype(BF16).astype(F32)
    return first, second, third


def kernel(
    emb, w_in, bias, w_out, scale_in, noise_in, rs_in,
    img_out, sc_out,
    x_buf, w_buf, b_buf, wo_buf, rs_buf, rs_pad, data, at, bb,
    acc_a, acc_b, parts, stat_own, stat_got,
    load_sem, ds_sem, dr_sem, qs_sem, qr_sem, ss_sem, sr_sem,
):
    row, col = lax.axis_index("row"), lax.axis_index("col")
    x, y, z, core = col // 2, (row // 2) % 4, (row // 8) * 2 + col % 2, row % 2
    line, member = y * 4 + z, x * 2 + core
    mates = []
    for dx, dc in ((2, 0), (2, 1), (1, 0), (1, 1), (3, 0), (3, 1), (0, 1)):
        mx, mc = (x + dx) % 4, (core + dc) % 2
        mates.append((mx * 2 + mc, device_of(mx, y, z, mc)))
    up = (line + member + 1) % LINES
    uy, uz = up // 4, up % 4
    uppers = [device_of(m // 2, uy, uz, m % 2) for m in range(MEMBERS)]
    lowers = []
    for m in range(MEMBERS):
        down = (line + LINES - 1 - m) % LINES
        lowers.append(device_of(m // 2, down // 4, down % 4, m % 2))
    across = []
    for d in range(1, LINES):
        there = ((y + d // 4) % 4, (z + d % 4) % 4)
        across.append((there[0] * 4 + there[1], device_of(x, there[0], there[1], core)))

    loads = []

    def load(src, dst):
        c = pltpu.make_async_copy(src, dst, load_sem.at[len(loads)])
        c.start()
        loads.append(c)
        return c

    chunks = INNER // NCHUNK
    load_rs = load(rs_in, rs_buf)
    load_x = [load(emb.at[pl.ds(0, HALF), :], x_buf.at[0])]
    load_w = [load(w_in.at[:, pl.ds(n * NCHUNK, NCHUNK)], w_buf.at[n]) for n in range(chunks)]
    load_b = load(bias, b_buf)
    load_wo = load(w_out, wo_buf)
    load_x.append(load(emb.at[pl.ds(HALF, HALF), :], x_buf.at[1]))

    barrier = pltpu.get_barrier_semaphore()
    partners = lowers + uppers + [d for _, d in mates + across]
    for device in partners:
        pl.semaphore_signal(barrier, inc=1, device_id=device, device_id_type=MESH)

    own = pl.ds(pl.multiple_of(member * HALF, HALF), HALF)

    def remote(src, dst, send, recv, device):
        return pltpu.make_async_remote_copy(
            src_ref=src, dst_ref=dst, send_sem=send, recv_sem=recv,
            device_id=device, device_id_type=MESH,
        )

    KINDS = ((0, FEAT, PROBE_ROWS), (0, 0, FEAT), (1, 0, GATHERED))

    def slot(place):
        return pl.ds(pl.multiple_of(place * HALF, HALF), HALF)

    def mate_copy(kind, i, receiving):
        half, start, count = KINDS[kind]
        place, device = mates[i]
        if not receiving:
            place = member
        return remote(
            data.at[2 + half, pl.ds(start, count), own],
            data.at[2 + half, pl.ds(start, count), slot(place)],
            ds_sem.at[kind, i], dr_sem.at[kind, place], device,
        )

    def column_copy(kind, m, receiving):
        half, start, count = KINDS[kind]
        place = m if receiving else member
        return remote(
            data.at[2 + half, pl.ds(start, count), own],
            data.at[half, pl.ds(start, count), slot(place)],
            ds_sem.at[kind, MEMBERS + m], dr_sem.at[kind, MEMBERS + place],
            uppers[m] if receiving else lowers[m],
        )

    def send_own(kind):
        for m in range(MEMBERS):
            column_copy(kind, m, False).start()
        for i in range(len(mates)):
            mate_copy(kind, i, False).start()

    def wait_rows(kind):
        for i in range(len(mates)):
            mate_copy(kind, i, True).wait_recv()

    def wait_columns(kind):
        for m in range(MEMBERS):
            column_copy(kind, m, True).wait_recv()

    load_rs.wait()
    rs_pad[...] = jnp.zeros_like(rs_pad)
    rs_pad[pl.ds(0, COLS), :] = rs_buf[...]
    for h in range(2):
        data[2 + h, pl.ds(FEAT, PROBE_ROWS), own] = rs_pad[:, pl.ds(h * HALF, HALF)].astype(BF16)
    acc_a[...] = jnp.zeros_like(acc_a)
    acc_b[...] = jnp.zeros_like(acc_b)

    for h in range(2):
        load_x[h].wait()
        total = jnp.zeros((FEAT, HALF), F32)
        for n in range(chunks):
            if h == 0:
                load_w[n].wait()
                if n == 0:
                    load_b.wait()
                    load_wo.wait()
            pre = jnp.dot(x_buf[h], w_buf[n], preferred_element_type=F32)
            hidden = gelu(pre + b_buf[:, pl.ds(n * NCHUNK, NCHUNK)]).astype(BF16)
            total += lax.dot_general(
                wo_buf[:, pl.ds(n * NCHUNK, NCHUNK)], hidden, (((1,), (1,)), ((), ())),
                preferred_element_type=F32,
            )
            if h == 0 and n == 0:
                pl.semaphore_wait(barrier, len(partners))
                send_own(0)
        data[2 + h, pl.ds(0, FEAT), own] = total.astype(BF16)
        send_own(1 + h)

    length = jnp.full((1, SPAN), scale_in[0], F32)
    unit = (1.0 / math.log(2.0)) / (length * length)
    level = lax.broadcasted_iota(jnp.int32, (FEAT, SPAN), 0)

    def extras(norm, at_norm, at_one):
        one, two, three = pieces_of(norm)
        out = jnp.where((level >= at_one) & (level < at_one + 3), 1.0, 0.0)
        for i, piece in enumerate((one, two, three)):
            out = jnp.where(level == at_norm + i, jnp.broadcast_to(piece, out.shape), out)
        return out

    def build_columns(half):
        wide = data[half, pl.ds(0, FEAT), :].astype(F32)
        norm = jnp.sum(wide * wide, axis=0, keepdims=True) * (unit * -0.5)
        for i, piece in enumerate(pieces_of(wide * unit)):
            bb[half, pl.ds(i * FEAT, FEAT), :] = piece.astype(BF16)
        bb[half, pl.ds(3 * FEAT, FEAT), :] = extras(norm, 0, 3).astype(BF16)

    def build_rows(h):
        wide = data[2 + h, pl.ds(0, FEAT), :].astype(F32)
        norm = jnp.sum(wide * wide, axis=0, keepdims=True) * (unit * -0.5)
        at[h, :, pl.ds(0, 128)] = jnp.concatenate([wide, wide], axis=0).T.astype(BF16)
        at[h, :, pl.ds(128, 128)] = jnp.concatenate([wide, extras(norm, 3, 0)], axis=0).T.astype(BF16)

    def strip(a, row0, rows, b, col0, cols, both=True):
        here = pl.ds(col0, cols)
        right = bb[b, :, here]
        down = jnp.zeros((PROBE_ROWS, cols), F32)
        for i in range(rows // SUB):
            part = pl.ds(row0 + i * SUB, SUB)
            power = jnp.dot(at[a, part, :], right, preferred_element_type=F32)
            tile = jnp.exp2(power).astype(BF16)
            down += jnp.dot(
                data[2 + a, pl.ds(FEAT, PROBE_ROWS), part], tile, preferred_element_type=F32
            )
            if both:
                acc_a[a, :, part] += lax.dot_general(
                    data[b, pl.ds(FEAT, PROBE_ROWS), here], tile,
                    (((1,), (1,)), ((), ())), preferred_element_type=F32,
                )
        acc_b[b, :, here] += down

    def quad(a, b, both=True):
        @pl.loop(0, SPAN // PIECE)
        def _(i):
            strip(a, 0, SPAN, b, pl.multiple_of(i * PIECE, PIECE), PIECE, both)

    special = member == MEMBERS - 1
    w = line // 8

    def row_part(half, m, receiving):
        place = m if receiving else member
        return remote(
            acc_a.at[half, pl.ds(0, SUM_ROWS), slot(m)], parts.at[half, place],
            qs_sem.at[half, m], qr_sem.at[half, place], device_of(m // 2, y, z, m % 2),
        )

    def column_part(half, m, receiving):
        place = MEMBERS + (m if receiving else member)
        device = lowers[m] if receiving else device_of(m // 2, uy, uz, m % 2)
        return remote(
            acc_b.at[half, pl.ds(0, SUM_ROWS), slot(m)], parts.at[half, place],
            qs_sem.at[half, MEMBERS + m], qr_sem.at[half, place], device,
        )

    def each_row_part(half, members, act):
        for m in members:
            @pl.when(member != m)
            def _():
                act(row_part(half, m, False))

    def each_column_part(half, members, act):
        for m in members:
            act(column_part(half, m, False))

    def start(c):
        c.start()

    def four(q):
        return [4 * q + i for i in range(4)]

    wait_rows(0)
    wait_rows(1)
    build_rows(0)

    @pl.when(special)
    def _():
        build_columns(2)
        quad(0, 2, False)

    wait_columns(0)
    wait_columns(1)
    build_columns(0)

    @pl.when(jnp.logical_not(special))
    def _():
        quad(0, 0)

    wait_rows(2)
    wait_columns(2)
    build_rows(1)
    build_columns(1)

    @pl.when(jnp.logical_not(special))
    def _():
        @pl.loop(0, 2)
        def _(q):
            at_piece = pl.multiple_of(q * PIECE, PIECE)
            strip(0, at_piece, PIECE, 1, 0, SPAN)
            each_row_part(0, four(q), start)
            strip(1, 0, SPAN, 0, at_piece, PIECE)
            each_column_part(0, four(q), start)

        strip(1, 0, PIECE, 1, 0, SPAN)
        each_row_part(1, four(0), start)

        @pl.loop(0, 2)
        def _(q):
            strip(1, PIECE, PIECE, 1, pl.multiple_of(q * PIECE, PIECE), PIECE)
            each_column_part(1, four(q), start)

        each_row_part(1, four(1), start)

    @pl.when(special)
    def _():
        quad(w, 0)
        each_column_part(0, range(MEMBERS), start)
        quad(1 - w, 1)
        each_column_part(1, range(MEMBERS), start)
        build_columns(3)
        quad(0, 3)
        acc_a[0] += acc_b[2]
        each_row_part(0, range(MEMBERS), start)
        quad(1, 3, False)
        acc_a[1] += acc_b[3]
        each_row_part(1, range(MEMBERS), start)

    for h in range(2):
        for m in range(MEMBERS):
            column_part(h, m, True).wait_recv()

            @pl.when(member != m)
            def _():
                row_part(h, m, True).wait_recv()

    right = [rs_pad[pl.ds(0, SUM_ROWS), pl.ds(h * HALF, HALF)] for h in range(2)]
    images = []
    for h in range(2):
        parts[h, member] = acc_a[h, pl.ds(0, SUM_ROWS), own]
        images.append(jnp.sum(parts[h], axis=0) + noise_in[0] * right[h])
        img_out[:, pl.ds(h * HALF, HALF)] = images[h][:COLS]

    def over(terms):
        return sum(jnp.sum(t, axis=1, keepdims=True) for t in terms)

    def ratio(top, bottom):
        return jnp.where(bottom > 0.0, top / jnp.where(bottom > 0.0, bottom, 1.0), 0.0)

    norm = over([r * r for r in right])
    curve = over([r * i for r, i in zip(right, images)])
    alpha = ratio(curve, norm)
    spread = over([(i - alpha * r) * (i - alpha * r) for r, i in zip(right, images)])
    lane = lax.broadcasted_iota(jnp.int32, (128, 128), 1)
    out = jnp.zeros((128, 128), F32)
    for i, v in enumerate((norm, curve, spread)):
        tall = jnp.concatenate([v, jnp.zeros((128 - SUM_ROWS, 1), F32)], axis=0)
        out = jnp.where(lane == i, jnp.broadcast_to(tall, out.shape), out)
    stat_own[0] = out.T[:8]

    level8 = lax.broadcasted_iota(jnp.int32, (8, 128), 0)

    def packed(values):
        out = jnp.zeros((8, 128), F32)
        for i, v in enumerate(values):
            out = jnp.where(level8 == i, jnp.broadcast_to(v, out.shape), out)
        return out

    def merged(stats):
        norms, curves, spreads = (stats[:, i : i + 1, :] for i in range(3))
        norm = jnp.sum(norms, axis=0)
        curve = jnp.sum(curves, axis=0)
        shift = ratio(curves, norms) - ratio(curve, norm)[None]
        return norm, curve, jnp.sum(spreads + norms * shift * shift, axis=0)

    stages = ((0, member, mates), (MEMBERS, line, across))

    def stat_copy(stage, i, receiving):
        base, mine, others = stages[stage]
        place, device = others[i]
        slot = base + (place if receiving else mine)
        return remote(
            stat_own.at[stage], stat_got.at[slot], ss_sem.at[base + i], sr_sem.at[slot], device
        )

    for stage, (base, mine, others) in enumerate(stages):
        for i in range(len(others)):
            stat_copy(stage, i, False).start()
        stat_got[base + mine] = stat_own[stage]
        for i in range(len(others)):
            stat_copy(stage, i, True).wait_recv()
        norm, curve, spread = merged(stat_got[pl.ds(base, len(others) + 1)])
        if stage < 1:
            stat_own[stage + 1] = packed((norm, curve, spread))
    step = norm / curve
    scalars = packed((step, step * step * spread / norm))
    sc_out[...] = jnp.concatenate([scalars, jnp.zeros((120, 128), F32)], axis=0).T[:COLS]

    def sent(c):
        c.wait_send()

    for kind in range(len(KINDS)):
        for i in range(len(mates)):
            mate_copy(kind, i, False).wait_send()
        for m in range(MEMBERS):
            column_copy(kind, m, False).wait_send()
    for h in range(2):
        each_row_part(h, range(MEMBERS), sent)
        each_column_part(h, range(MEMBERS), sent)
    for stage, (_, _, others) in enumerate(stages):
        for i in range(len(others)):
            stat_copy(stage, i, False).wait_send()


def on_device(embeddings, weight_in, bias_in, weight_out, lengthscale, noise_level, right_side):
    anywhere = pl.BlockSpec(memory_space=pl.ANY)
    scalar = pl.BlockSpec(memory_space=pltpu.SMEM)
    vmem = pl.BlockSpec(memory_space=pltpu.VMEM)
    dma = pltpu.SemaphoreType.DMA
    images, scalars = pl.pallas_call(
        kernel,
        out_shape=(
            jax.ShapeDtypeStruct((COLS, BLOCK), F32),
            jax.ShapeDtypeStruct((COLS, 128), F32),
        ),
        in_specs=[anywhere, anywhere, anywhere, anywhere, scalar, scalar, anywhere],
        out_specs=[vmem, vmem],
        scratch_shapes=[
            pltpu.VMEM((2, HALF, EMBED), BF16),
            pltpu.VMEM((INNER // NCHUNK, EMBED, NCHUNK), BF16),
            pltpu.VMEM((1, INNER), F32),
            pltpu.VMEM((FEAT, INNER), BF16),
            pltpu.VMEM((COLS, BLOCK), F32),
            pltpu.VMEM((PROBE_ROWS, BLOCK), F32),
            pltpu.VMEM((4, GATHERED, SPAN), BF16),
            pltpu.VMEM((2, SPAN, 256), BF16),
            pltpu.VMEM((4, 256, SPAN), BF16),
            pltpu.VMEM((2, PROBE_ROWS, SPAN), F32),
            pltpu.VMEM((4, PROBE_ROWS, SPAN), F32),
            pltpu.VMEM((2, 2 * MEMBERS, SUM_ROWS, HALF), F32),
            pltpu.VMEM((2, 8, 128), F32),
            pltpu.VMEM((MEMBERS + LINES, 8, 128), F32),
            dma((9,)),
            dma((3, 2 * MEMBERS)),
            dma((3, 2 * MEMBERS)),
            dma((2, 2 * MEMBERS)),
            dma((2, 2 * MEMBERS)),
            dma((MEMBERS + LINES,)),
            dma((MEMBERS + LINES,)),
        ],
        compiler_params=pltpu.CompilerParams(
            collective_id=0, has_side_effects=True, vmem_limit_bytes=56 * 2**20
        ),
        name="cg_step",
    )(
        embeddings, weight_in, bias_in.reshape(1, INNER), weight_out.T, lengthscale, noise_level,
        right_side,
    )
    step_size = scalars[:, 0]
    correction = scalars[:, 1]
    residual = right_side - step_size[:, None] * images
    direction = residual + correction[:, None] * right_side
    return (residual, direction, step_size, correction)


def solution(mesh):
    in_specs = (P(("row", "col"), None), P(), P(), P(), P(), P(), P(None, ("row", "col")))
    out_specs = (P(None, ("row", "col")), P(None, ("row", "col")), P(), P())
    return jax.shard_map(
        on_device, mesh=mesh, in_specs=in_specs, out_specs=out_specs, check_vma=False
    )
```

```python
import functools
import math

import jax
import jax.numpy as jnp
from jax import lax
from jax.experimental import pallas as pl
from jax.experimental.pallas import tpu as pltpu
from jax.sharding import PartitionSpec as P

MESH = pl.DeviceIdType.MESH
F32 = jnp.float32
BF16 = jnp.bfloat16

LINES = 16
MEMBERS = 8
BLOCK = 512
HALF = 256
SPAN = MEMBERS * HALF
FEAT = 64
GATHERED = FEAT + 48
EMBED = 2560
INNER = 1024
COLS = 33
PROBE_ROWS = 48
SUM_ROWS = 40
PIECE = 1024
SUB = 512
NCHUNK = 256


def device_of(x, y, z, core):
    return ((z // 2) * 8 + y * 2 + core, x * 2 + z % 2)


def gelu(v):
    return 0.5 * v * (1.0 + lax.erf(v * (1.0 / math.sqrt(2.0))))


def pieces_of(v):
    first = v.astype(BF16).astype(F32)
    rest = v - first
    second = rest.astype(BF16).astype(F32)
    third = (rest - second).astype(BF16).astype(F32)
    return first, second, third


def kernel(
    emb, w_in, bias, w_out, scale_in, noise_in, rs_in,
    img_out, sc_out,
    x_buf, w_buf, b_buf, wo_buf, rs_buf, rs_pad, data, at, bb,
    acc_a, acc_b, parts, stat_own, stat_got,
    load_sem, ds_sem, dr_sem, qs_sem, qr_sem, ss_sem, sr_sem,
):
    row, col = lax.axis_index("row"), lax.axis_index("col")
    x, y, z, core = col // 2, (row // 2) % 4, (row // 8) * 2 + col % 2, row % 2
    line, member = y * 4 + z, x * 2 + core
    mates = []
    for dx, dc in ((2, 0), (2, 1), (1, 0), (1, 1), (3, 0), (3, 1), (0, 1)):
        mx, mc = (x + dx) % 4, (core + dc) % 2
        mates.append((mx * 2 + mc, device_of(mx, y, z, mc)))
    up = (line + member + 1) % LINES
    uy, uz = up // 4, up % 4
    uppers = [device_of(m // 2, uy, uz, m % 2) for m in range(MEMBERS)]
    lowers = []
    for m in range(MEMBERS):
        down = (line + LINES - 1 - m) % LINES
        lowers.append(device_of(m // 2, down // 4, down % 4, m % 2))
    targets = []
    for dx in range(4):
        tx = (x + dx) % 4
        for tc in range(2):
            down = (line + LINES - 1 - tx * 2 - tc) % LINES
            targets.append(device_of(tx, down // 4, down % 4, tc))
    sibling = device_of(x, y, z, 1 - core)
    peers = [((x + dx) % 4, device_of((x + dx) % 4, y, z, core)) for dx in (2, 1, 3)]
    across = []
    for d in range(1, LINES):
        there = ((y + d // 4) % 4, (z + d % 4) % 4)
        across.append((there[0] * 4 + there[1], device_of(x, there[0], there[1], core)))

    loads = []

    def load(src, dst):
        c = pltpu.make_async_copy(src, dst, load_sem.at[len(loads)])
        c.start()
        loads.append(c)
        return c

    chunks = INNER // NCHUNK
    load_rs = load(rs_in, rs_buf)
    load_x = [load(emb.at[pl.ds(0, HALF), :], x_buf.at[0])]
    load_w = [load(w_in.at[:, pl.ds(n * NCHUNK, NCHUNK)], w_buf.at[n]) for n in range(chunks)]
    load_b = load(bias, b_buf)
    load_wo = load(w_out, wo_buf)
    load_x.append(load(emb.at[pl.ds(HALF, HALF), :], x_buf.at[1]))

    barrier = pltpu.get_barrier_semaphore()
    partners = lowers + uppers + [d for _, d in mates + across]
    for device in partners:
        pl.semaphore_signal(barrier, inc=1, device_id=device, device_id_type=MESH)

    own = pl.ds(pl.multiple_of(member * HALF, HALF), HALF)

    def remote(src, dst, send, recv, device):
        return pltpu.make_async_remote_copy(
            src_ref=src, dst_ref=dst, send_sem=send, recv_sem=recv,
            device_id=device, device_id_type=MESH,
        )

    KINDS = ((0, FEAT, PROBE_ROWS), (0, 0, FEAT), (1, 0, GATHERED))

    def slot(place):
        return pl.ds(pl.multiple_of(place * HALF, HALF), HALF)

    def data_copy(kind, place, to_rows, send_at, device):
        half, start, count = KINDS[kind]
        rows = pl.ds(start, count)
        return remote(
            data.at[2 + half, rows, slot(place)],
            data.at[half + (2 if to_rows else 0), rows, slot(place)],
            ds_sem.at[kind, send_at],
            dr_sem.at[kind, place if to_rows else MEMBERS + place], device,
        )

    def own_copies(kind):
        if kind == 2:
            rows = [
                data_copy(kind, member, True, 8 + i, device) for i, (_, device) in enumerate(mates)
            ]
            return rows + [data_copy(kind, member, False, i, targets[i]) for i in range(8)]
        near = [data_copy(kind, member, False, i, targets[i]) for i in (4, 5, 2, 3, 6, 7, 0, 1)]
        line_copies = [
            data_copy(kind, member, True, 8 + i, device) for i, (_, device) in enumerate(peers)
        ]
        return line_copies + near + [data_copy(kind, member, True, 11, sibling)]

    def passed_copies(kind, i):
        place = peers[i][0] * 2 + core
        copies = [data_copy(kind, place, True, 12 + i, sibling)]
        return copies

    def send_own(kind):
        for c in own_copies(kind):
            c.start()

    def pass_on(kind):
        for i in range(len(peers)):
            data_copy(kind, peers[i][0] * 2 + core, True, 8 + i, sibling).wait_recv()
            for c in passed_copies(kind, i):
                c.start()

    def wait_rows(kind):
        if kind == 2:
            for i, (place, device) in enumerate(mates):
                data_copy(kind, place, True, 8 + i, device).wait_recv()
            return
        for dx in range(4):
            data_copy(kind, (x + dx) % 4 * 2 + 1 - core, True, 11, sibling).wait_recv()

    def wait_columns(kind):
        for m in range(MEMBERS):
            data_copy(kind, m, False, m, uppers[m]).wait_recv()

    load_rs.wait()
    rs_pad[...] = jnp.zeros_like(rs_pad)
    rs_pad[pl.ds(0, COLS), :] = rs_buf[...]
    for h in range(2):
        data[2 + h, pl.ds(FEAT, PROBE_ROWS), own] = rs_pad[:, pl.ds(h * HALF, HALF)].astype(BF16)
    acc_a[...] = jnp.zeros_like(acc_a)
    acc_b[...] = jnp.zeros_like(acc_b)

    for h in range(2):
        load_x[h].wait()
        total = jnp.zeros((FEAT, HALF), F32)
        for n in range(chunks):
            if h == 0:
                load_w[n].wait()
                if n == 0:
                    load_b.wait()
                    load_wo.wait()
            pre = jnp.dot(x_buf[h], w_buf[n], preferred_element_type=F32)
            hidden = gelu(pre + b_buf[:, pl.ds(n * NCHUNK, NCHUNK)]).astype(BF16)
            total += lax.dot_general(
                wo_buf[:, pl.ds(n * NCHUNK, NCHUNK)], hidden, (((1,), (1,)), ((), ())),
                preferred_element_type=F32,
            )
            if h == 0 and n == 0:
                pl.semaphore_wait(barrier, len(partners))
                send_own(0)
        data[2 + h, pl.ds(0, FEAT), own] = total.astype(BF16)
        send_own(1 + h)

    length = jnp.full((1, SPAN), scale_in[0], F32)
    unit = (1.0 / math.log(2.0)) / (length * length)
    level = lax.broadcasted_iota(jnp.int32, (FEAT, SPAN), 0)

    def extras(norm, at_norm, at_one):
        one, two, three = pieces_of(norm)
        out = jnp.where((level >= at_one) & (level < at_one + 3), 1.0, 0.0)
        for i, piece in enumerate((one, two, three)):
            out = jnp.where(level == at_norm + i, jnp.broadcast_to(piece, out.shape), out)
        return out

    def build_columns(half):
        wide = data[half, pl.ds(0, FEAT), :].astype(F32)
        norm = jnp.sum(wide * wide, axis=0, keepdims=True) * (unit * -0.5)
        for i, piece in enumerate(pieces_of(wide * unit)):
            bb[half, pl.ds(i * FEAT, FEAT), :] = piece.astype(BF16)
        bb[half, pl.ds(3 * FEAT, FEAT), :] = extras(norm, 0, 3).astype(BF16)

    def build_rows(h):
        wide = data[2 + h, pl.ds(0, FEAT), :].astype(F32)
        norm = jnp.sum(wide * wide, axis=0, keepdims=True) * (unit * -0.5)
        at[h, :, pl.ds(0, 128)] = jnp.concatenate([wide, wide], axis=0).T.astype(BF16)
        at[h, :, pl.ds(128, 128)] = jnp.concatenate([wide, extras(norm, 3, 0)], axis=0).T.astype(BF16)

    def strip(a, row0, rows, b, col0, cols, both=True):
        here = pl.ds(col0, cols)
        right = bb[b, :, here]
        down = jnp.zeros((PROBE_ROWS, cols), F32)
        for i in range(rows // SUB):
            part = pl.ds(row0 + i * SUB, SUB)
            power = jnp.dot(at[a, part, :], right, preferred_element_type=F32)
            tile = jnp.exp2(power).astype(BF16)
            down += jnp.dot(
                data[2 + a, pl.ds(FEAT, PROBE_ROWS), part], tile, preferred_element_type=F32
            )
            if both:
                acc_a[a, :, part] += lax.dot_general(
                    data[b, pl.ds(FEAT, PROBE_ROWS), here], tile,
                    (((1,), (1,)), ((), ())), preferred_element_type=F32,
                )
        acc_b[b, :, here] += down

    def quad(a, b, both=True):
        @pl.loop(0, SPAN // PIECE)
        def _(i):
            strip(a, 0, SPAN, b, pl.multiple_of(i * PIECE, PIECE), PIECE, both)

    special = member == MEMBERS - 1
    w = line // 8

    def row_part(half, m, receiving):
        place = m if receiving else member
        return remote(
            acc_a.at[half, pl.ds(0, SUM_ROWS), slot(m)], parts.at[half, place],
            qs_sem.at[half, m], qr_sem.at[half, place], device_of(m // 2, y, z, m % 2),
        )

    def column_part(half, m, receiving):
        place = MEMBERS + (m if receiving else member)
        device = lowers[m] if receiving else device_of(m // 2, uy, uz, m % 2)
        return remote(
            acc_b.at[half, pl.ds(0, SUM_ROWS), slot(m)], parts.at[half, place],
            qs_sem.at[half, MEMBERS + m], qr_sem.at[half, place], device,
        )

    def each_row_part(half, members, act):
        for m in members:
            @pl.when(member != m)
            def _():
                act(row_part(half, m, False))

    def each_column_part(half, members, act):
        for m in members:
            act(column_part(half, m, False))

    def start(c):
        c.start()

    def four(q):
        return [4 * q + i for i in range(4)]

    pass_on(0)
    pass_on(1)
    wait_rows(0)
    wait_rows(1)
    build_rows(0)

    @pl.when(special)
    def _():
        build_columns(2)
        quad(0, 2, False)

    wait_columns(0)
    wait_columns(1)
    build_columns(0)

    @pl.when(jnp.logical_not(special))
    def _():
        strip(0, 0, SPAN, 0, 0, PIECE)

    @pl.when(jnp.logical_not(special))
    def _():
        strip(0, 0, SPAN, 0, PIECE, PIECE)

    wait_rows(2)
    build_rows(1)

    @pl.when(jnp.logical_not(special))
    def _():
        for q in range(2):
            strip(1, 0, SPAN, 0, q * PIECE, PIECE)
            each_column_part(0, four(q), start)

    wait_columns(2)
    build_columns(1)

    @pl.when(jnp.logical_not(special))
    def _():
        for q in range(2):
            strip(0, q * PIECE, PIECE, 1, 0, SPAN)
            each_row_part(0, four(q), start)
        strip(1, 0, PIECE, 1, 0, SPAN)
        each_row_part(1, four(0), start)

        @pl.loop(0, 2)
        def _(q):
            strip(1, PIECE, PIECE, 1, pl.multiple_of(q * PIECE, PIECE), PIECE)
            each_column_part(1, four(q), start)

        each_row_part(1, four(1), start)

    @pl.when(special)
    def _():
        quad(w, 0)
        each_column_part(0, range(MEMBERS), start)
        quad(1 - w, 1)
        each_column_part(1, range(MEMBERS), start)
        build_columns(3)
        quad(0, 3)
        acc_a[0] += acc_b[2]
        each_row_part(0, range(MEMBERS), start)
        quad(1, 3, False)
        acc_a[1] += acc_b[3]
        each_row_part(1, range(MEMBERS), start)

    for h in range(2):
        for m in range(MEMBERS):
            column_part(h, m, True).wait_recv()

            @pl.when(member != m)
            def _():
                row_part(h, m, True).wait_recv()

    right = [rs_pad[pl.ds(0, SUM_ROWS), pl.ds(h * HALF, HALF)] for h in range(2)]
    images = []
    for h in range(2):
        parts[h, member] = acc_a[h, pl.ds(0, SUM_ROWS), own]
        images.append(jnp.sum(parts[h], axis=0) + noise_in[0] * right[h])
        img_out[:, pl.ds(h * HALF, HALF)] = images[h][:COLS]

    def over(terms):
        return sum(jnp.sum(t, axis=1, keepdims=True) for t in terms)

    def ratio(top, bottom):
        return jnp.where(bottom > 0.0, top / jnp.where(bottom > 0.0, bottom, 1.0), 0.0)

    norm = over([r * r for r in right])
    curve = over([r * i for r, i in zip(right, images)])
    alpha = ratio(curve, norm)
    spread = over([(i - alpha * r) * (i - alpha * r) for r, i in zip(right, images)])
    lane = lax.broadcasted_iota(jnp.int32, (128, 128), 1)
    out = jnp.zeros((128, 128), F32)
    for i, v in enumerate((norm, curve, spread)):
        tall = jnp.concatenate([v, jnp.zeros((128 - SUM_ROWS, 1), F32)], axis=0)
        out = jnp.where(lane == i, jnp.broadcast_to(tall, out.shape), out)
    stat_own[0] = out.T[:8]

    level8 = lax.broadcasted_iota(jnp.int32, (8, 128), 0)

    def packed(values):
        out = jnp.zeros((8, 128), F32)
        for i, v in enumerate(values):
            out = jnp.where(level8 == i, jnp.broadcast_to(v, out.shape), out)
        return out

    def merged(stats):
        norms, curves, spreads = (stats[:, i : i + 1, :] for i in range(3))
        norm = jnp.sum(norms, axis=0)
        curve = jnp.sum(curves, axis=0)
        shift = ratio(curves, norms) - ratio(curve, norm)[None]
        return norm, curve, jnp.sum(spreads + norms * shift * shift, axis=0)

    stages = ((0, member, mates), (MEMBERS, line, across))

    def stat_copy(stage, i, receiving):
        base, mine, others = stages[stage]
        place, device = others[i]
        slot = base + (place if receiving else mine)
        return remote(
            stat_own.at[stage], stat_got.at[slot], ss_sem.at[base + i], sr_sem.at[slot], device
        )

    for stage, (base, mine, others) in enumerate(stages):
        for i in range(len(others)):
            stat_copy(stage, i, False).start()
        stat_got[base + mine] = stat_own[stage]
        for i in range(len(others)):
            stat_copy(stage, i, True).wait_recv()
        norm, curve, spread = merged(stat_got[pl.ds(base, len(others) + 1)])
        if stage < 1:
            stat_own[stage + 1] = packed((norm, curve, spread))
    step = norm / curve
    scalars = packed((step, step * step * spread / norm))
    sc_out[...] = jnp.concatenate([scalars, jnp.zeros((120, 128), F32)], axis=0).T[:COLS]

    def sent(c):
        c.wait_send()

    for kind in range(len(KINDS)):
        for c in own_copies(kind) + (
            sum((passed_copies(kind, i) for i in range(len(peers))), []) if kind < 2 else []
        ):
            c.wait_send()
    for h in range(2):
        each_row_part(h, range(MEMBERS), sent)
        each_column_part(h, range(MEMBERS), sent)
    for stage, (_, _, others) in enumerate(stages):
        for i in range(len(others)):
            stat_copy(stage, i, False).wait_send()


def on_device(embeddings, weight_in, bias_in, weight_out, lengthscale, noise_level, right_side):
    anywhere = pl.BlockSpec(memory_space=pl.ANY)
    scalar = pl.BlockSpec(memory_space=pltpu.SMEM)
    vmem = pl.BlockSpec(memory_space=pltpu.VMEM)
    dma = pltpu.SemaphoreType.DMA
    images, scalars = pl.pallas_call(
        kernel,
        out_shape=(
            jax.ShapeDtypeStruct((COLS, BLOCK), F32),
            jax.ShapeDtypeStruct((COLS, 128), F32),
        ),
        in_specs=[anywhere, anywhere, anywhere, anywhere, scalar, scalar, anywhere],
        out_specs=[vmem, vmem],
        scratch_shapes=[
            pltpu.VMEM((2, HALF, EMBED), BF16),
            pltpu.VMEM((INNER // NCHUNK, EMBED, NCHUNK), BF16),
            pltpu.VMEM((1, INNER), F32),
            pltpu.VMEM((FEAT, INNER), BF16),
            pltpu.VMEM((COLS, BLOCK), F32),
            pltpu.VMEM((PROBE_ROWS, BLOCK), F32),
            pltpu.VMEM((4, GATHERED, SPAN), BF16),
            pltpu.VMEM((2, SPAN, 256), BF16),
            pltpu.VMEM((4, 256, SPAN), BF16),
            pltpu.VMEM((2, PROBE_ROWS, SPAN), F32),
            pltpu.VMEM((4, PROBE_ROWS, SPAN), F32),
            pltpu.VMEM((2, 2 * MEMBERS, SUM_ROWS, HALF), F32),
            pltpu.VMEM((2, 8, 128), F32),
            pltpu.VMEM((MEMBERS + LINES, 8, 128), F32),
            dma((9,)),
            dma((3, 2 * MEMBERS)),
            dma((3, 2 * MEMBERS)),
            dma((2, 2 * MEMBERS)),
            dma((2, 2 * MEMBERS)),
            dma((MEMBERS + LINES,)),
            dma((MEMBERS + LINES,)),
        ],
        compiler_params=pltpu.CompilerParams(
            collective_id=0, has_side_effects=True, vmem_limit_bytes=56 * 2**20
        ),
        name="cg_step",
    )(
        embeddings, weight_in, bias_in.reshape(1, INNER), weight_out.T, lengthscale, noise_level,
        right_side,
    )
    step_size = scalars[:, 0]
    correction = scalars[:, 1]
    residual = right_side - step_size[:, None] * images
    direction = residual + correction[:, None] * right_side
    return (residual, direction, step_size, correction)


def solution(mesh):
    in_specs = (P(("row", "col"), None), P(), P(), P(), P(), P(), P(None, ("row", "col")))
    out_specs = (P(None, ("row", "col")), P(None, ("row", "col")), P(), P())
    return jax.shard_map(
        on_device, mesh=mesh, in_specs=in_specs, out_specs=out_specs, check_vma=False
    )
```

```python
import functools
import math

import jax
import jax.numpy as jnp
from jax import lax
from jax.experimental import pallas as pl
from jax.experimental.pallas import tpu as pltpu
from jax.sharding import PartitionSpec as P

MESH = pl.DeviceIdType.MESH
F32 = jnp.float32
BF16 = jnp.bfloat16

LINES = 16
MEMBERS = 8
BLOCK = 512
HALF = 256
SPAN = MEMBERS * HALF
FEAT = 64
GATHERED = FEAT + 48
EMBED = 2560
INNER = 1024
COLS = 33
PROBE_ROWS = 48
SUM_ROWS = 40
PIECE = 1024
SUB = 512
NCHUNK = 256


def device_of(x, y, z, core):
    return ((z // 2) * 8 + y * 2 + core, x * 2 + z % 2)


def gelu(v):
    return 0.5 * v * (1.0 + lax.erf(v * (1.0 / math.sqrt(2.0))))


def pieces_of(v):
    first = v.astype(BF16).astype(F32)
    rest = v - first
    second = rest.astype(BF16).astype(F32)
    third = (rest - second).astype(BF16).astype(F32)
    return first, second, third


def kernel(
    emb, w_in, bias, w_out, scale_in, noise_in, rs_in,
    img_out, sc_out,
    x_buf, w_buf, b_buf, wo_buf, rs_buf, rs_pad, data, at, bb,
    acc_a, acc_b, parts, stat_own, stat_got,
    load_sem, ds_sem, dr_sem, qs_sem, qr_sem, ss_sem, sr_sem,
):
    row, col = lax.axis_index("row"), lax.axis_index("col")
    x, y, z, core = col // 2, (row // 2) % 4, (row // 8) * 2 + col % 2, row % 2
    line, member = y * 4 + z, x * 2 + core
    mates = []
    for dx, dc in ((2, 0), (2, 1), (1, 0), (1, 1), (3, 0), (3, 1), (0, 1)):
        mx, mc = (x + dx) % 4, (core + dc) % 2
        mates.append((mx * 2 + mc, device_of(mx, y, z, mc)))
    up = (line + member + 1) % LINES
    uy, uz = up // 4, up % 4
    uppers = [device_of(m // 2, uy, uz, m % 2) for m in range(MEMBERS)]
    lowers = []
    for m in range(MEMBERS):
        down = (line + LINES - 1 - m) % LINES
        lowers.append(device_of(m // 2, down // 4, down % 4, m % 2))
    targets = []
    for dx in range(4):
        tx = (x + dx) % 4
        for tc in range(2):
            down = (line + LINES - 1 - tx * 2 - tc) % LINES
            targets.append(device_of(tx, down // 4, down % 4, tc))
    sibling = device_of(x, y, z, 1 - core)
    peers = [((x + dx) % 4, device_of((x + dx) % 4, y, z, core)) for dx in (2, 1, 3)]
    across = []
    for d in range(1, LINES):
        there = ((y + d // 4) % 4, (z + d % 4) % 4)
        across.append((there[0] * 4 + there[1], device_of(x, there[0], there[1], core)))

    loads = []

    def load(src, dst):
        c = pltpu.make_async_copy(src, dst, load_sem.at[len(loads)])
        c.start()
        loads.append(c)
        return c

    chunks = INNER // NCHUNK
    load_rs = load(rs_in, rs_buf)
    load_x = [load(emb.at[pl.ds(0, HALF), :], x_buf.at[0])]
    load_w = [load(w_in.at[:, pl.ds(n * NCHUNK, NCHUNK)], w_buf.at[n]) for n in range(chunks)]
    load_b = load(bias, b_buf)
    load_wo = load(w_out, wo_buf)
    load_x.append(load(emb.at[pl.ds(HALF, HALF), :], x_buf.at[1]))

    barrier = pltpu.get_barrier_semaphore()
    partners = lowers + uppers + [d for _, d in mates + across]
    for device in partners:
        pl.semaphore_signal(barrier, inc=1, device_id=device, device_id_type=MESH)

    own = pl.ds(pl.multiple_of(member * HALF, HALF), HALF)

    def remote(src, dst, send, recv, device):
        return pltpu.make_async_remote_copy(
            src_ref=src, dst_ref=dst, send_sem=send, recv_sem=recv,
            device_id=device, device_id_type=MESH,
        )

    KINDS = ((0, FEAT, PROBE_ROWS), (0, 0, FEAT), (1, 0, GATHERED))

    def slot(place):
        return pl.ds(pl.multiple_of(place * HALF, HALF), HALF)

    def data_copy(kind, place, to_rows, send_at, device):
        half, start, count = KINDS[kind]
        rows = pl.ds(start, count)
        return remote(
            data.at[2 + half, rows, slot(place)],
            data.at[half + (2 if to_rows else 0), rows, slot(place)],
            ds_sem.at[kind, send_at],
            dr_sem.at[kind, place if to_rows else MEMBERS + place], device,
        )

    def own_copies(kind):
        if kind == 2:
            rows = [
                data_copy(kind, member, True, 8 + i, device) for i, (_, device) in enumerate(mates)
            ]
            return rows + [data_copy(kind, member, False, i, targets[i]) for i in range(8)]
        near = [data_copy(kind, member, False, i, targets[i]) for i in (4, 5, 2, 3, 6, 7, 0, 1)]
        line_copies = [
            data_copy(kind, member, True, 8 + i, device) for i, (_, device) in enumerate(peers)
        ]
        return line_copies + near + [data_copy(kind, member, True, 11, sibling)]

    def passed_copies(kind, i):
        place = peers[i][0] * 2 + core
        copies = [data_copy(kind, place, True, 12 + i, sibling)]
        return copies

    def send_own(kind):
        for c in own_copies(kind):
            c.start()

    def pass_on(kind):
        for i in range(len(peers)):
            data_copy(kind, peers[i][0] * 2 + core, True, 8 + i, sibling).wait_recv()
            for c in passed_copies(kind, i):
                c.start()

    def wait_rows(kind):
        if kind == 2:
            for i, (place, device) in enumerate(mates):
                data_copy(kind, place, True, 8 + i, device).wait_recv()
            return
        for dx in range(4):
            data_copy(kind, (x + dx) % 4 * 2 + 1 - core, True, 11, sibling).wait_recv()

    def wait_columns(kind):
        for m in range(MEMBERS):
            data_copy(kind, m, False, m, uppers[m]).wait_recv()

    load_rs.wait()
    rs_pad[...] = jnp.zeros_like(rs_pad)
    rs_pad[pl.ds(0, COLS), :] = rs_buf[...]
    for h in range(2):
        data[2 + h, pl.ds(FEAT, PROBE_ROWS), own] = rs_pad[:, pl.ds(h * HALF, HALF)].astype(BF16)
    acc_a[...] = jnp.zeros_like(acc_a)
    acc_b[...] = jnp.zeros_like(acc_b)

    for h in range(2):
        load_x[h].wait()
        total = jnp.zeros((FEAT, HALF), F32)
        for n in range(chunks):
            if h == 0:
                load_w[n].wait()
                if n == 0:
                    load_b.wait()
                    load_wo.wait()
            pre = jnp.dot(x_buf[h], w_buf[n], preferred_element_type=F32)
            hidden = gelu(pre + b_buf[:, pl.ds(n * NCHUNK, NCHUNK)]).astype(BF16)
            total += lax.dot_general(
                wo_buf[:, pl.ds(n * NCHUNK, NCHUNK)], hidden, (((1,), (1,)), ((), ())),
                preferred_element_type=F32,
            )
            if h == 0 and n == 0:
                pl.semaphore_wait(barrier, len(partners))
                send_own(0)
        data[2 + h, pl.ds(0, FEAT), own] = total.astype(BF16)
        send_own(1 + h)

    length = jnp.full((1, SPAN), scale_in[0], F32)
    unit = (1.0 / math.log(2.0)) / (length * length)
    level = lax.broadcasted_iota(jnp.int32, (FEAT, SPAN), 0)

    def extras(norm, at_norm, at_one):
        one, two, three = pieces_of(norm)
        out = jnp.where((level >= at_one) & (level < at_one + 3), 1.0, 0.0)
        for i, piece in enumerate((one, two, three)):
            out = jnp.where(level == at_norm + i, jnp.broadcast_to(piece, out.shape), out)
        return out

    def build_columns(half):
        wide = data[half, pl.ds(0, FEAT), :].astype(F32)
        norm = jnp.sum(wide * wide, axis=0, keepdims=True) * (unit * -0.5)
        for i, piece in enumerate(pieces_of(wide * unit)):
            bb[half, pl.ds(i * FEAT, FEAT), :] = piece.astype(BF16)
        bb[half, pl.ds(3 * FEAT, FEAT), :] = extras(norm, 0, 3).astype(BF16)

    def build_rows(h):
        wide = data[2 + h, pl.ds(0, FEAT), :].astype(F32)
        norm = jnp.sum(wide * wide, axis=0, keepdims=True) * (unit * -0.5)
        at[h, :, pl.ds(0, 128)] = jnp.concatenate([wide, wide], axis=0).T.astype(BF16)
        at[h, :, pl.ds(128, 128)] = jnp.concatenate([wide, extras(norm, 3, 0)], axis=0).T.astype(BF16)

    def strip(a, row0, rows, b, col0, cols, both=True):
        here = pl.ds(col0, cols)
        right = bb[b, :, here]
        down = jnp.zeros((PROBE_ROWS, cols), F32)
        for i in range(rows // SUB):
            part = pl.ds(row0 + i * SUB, SUB)
            power = jnp.dot(at[a, part, :], right, preferred_element_type=F32)
            tile = jnp.exp2(power).astype(BF16)
            down += jnp.dot(
                data[2 + a, pl.ds(FEAT, PROBE_ROWS), part], tile, preferred_element_type=F32
            )
            if both:
                acc_a[a, :, part] += lax.dot_general(
                    data[b, pl.ds(FEAT, PROBE_ROWS), here], tile,
                    (((1,), (1,)), ((), ())), preferred_element_type=F32,
                )
        acc_b[b, :, here] += down

    def quad(a, b, both=True):
        @pl.loop(0, SPAN // PIECE)
        def _(i):
            strip(a, 0, SPAN, b, pl.multiple_of(i * PIECE, PIECE), PIECE, both)

    special = member == MEMBERS - 1
    w = line // 8

    def row_part(half, m, receiving):
        place = m if receiving else member
        return remote(
            acc_a.at[half, pl.ds(0, SUM_ROWS), slot(m)], parts.at[half, place],
            qs_sem.at[half, m], qr_sem.at[half, place], device_of(m // 2, y, z, m % 2),
        )

    def column_part(half, m, receiving):
        place = MEMBERS + (m if receiving else member)
        device = lowers[m] if receiving else device_of(m // 2, uy, uz, m % 2)
        return remote(
            acc_b.at[half, pl.ds(0, SUM_ROWS), slot(m)], parts.at[half, place],
            qs_sem.at[half, MEMBERS + m], qr_sem.at[half, place], device,
        )

    def each_row_part(half, members, act):
        for m in members:
            @pl.when(member != m)
            def _():
                act(row_part(half, m, False))

    def each_column_part(half, members, act):
        for m in members:
            act(column_part(half, m, False))

    def start(c):
        c.start()

    def four(q):
        return [4 * q + i for i in range(4)]

    pass_on(0)
    pass_on(1)
    wait_rows(0)
    wait_rows(1)
    build_rows(0)

    @pl.when(special)
    def _():
        build_columns(2)
        quad(0, 2, False)

    wait_columns(0)
    wait_columns(1)
    build_columns(0)

    @pl.when(jnp.logical_not(special))
    def _():
        quad(0, 0)

    wait_rows(2)
    build_rows(1)

    @pl.when(jnp.logical_not(special))
    def _():
        @pl.loop(0, 2)
        def _(q):
            strip(1, 0, SPAN, 0, pl.multiple_of(q * PIECE, PIECE), PIECE)
            each_column_part(0, four(q), start)

    wait_columns(2)
    build_columns(1)

    @pl.when(jnp.logical_not(special))
    def _():
        @pl.loop(0, 2)
        def _(q):
            strip(0, pl.multiple_of(q * PIECE, PIECE), PIECE, 1, 0, SPAN)
            each_row_part(0, four(q), start)
        strip(1, 0, PIECE, 1, 0, SPAN)
        each_row_part(1, four(0), start)

        @pl.loop(0, 2)
        def _(q):
            strip(1, PIECE, PIECE, 1, pl.multiple_of(q * PIECE, PIECE), PIECE)
            each_column_part(1, four(q), start)

        each_row_part(1, four(1), start)

    @pl.when(special)
    def _():
        quad(w, 0)
        each_column_part(0, range(MEMBERS), start)
        quad(1 - w, 1)
        each_column_part(1, range(MEMBERS), start)
        build_columns(3)
        quad(0, 3)
        acc_a[0] += acc_b[2]
        each_row_part(0, range(MEMBERS), start)
        quad(1, 3, False)
        acc_a[1] += acc_b[3]
        each_row_part(1, range(MEMBERS), start)

    for h in range(2):
        for m in range(MEMBERS):
            column_part(h, m, True).wait_recv()

            @pl.when(member != m)
            def _():
                row_part(h, m, True).wait_recv()

    right = [rs_pad[pl.ds(0, SUM_ROWS), pl.ds(h * HALF, HALF)] for h in range(2)]
    images = []
    for h in range(2):
        parts[h, member] = acc_a[h, pl.ds(0, SUM_ROWS), own]
        images.append(jnp.sum(parts[h], axis=0) + noise_in[0] * right[h])
        img_out[:, pl.ds(h * HALF, HALF)] = images[h][:COLS]

    def over(terms):
        return sum(jnp.sum(t, axis=1, keepdims=True) for t in terms)

    def ratio(top, bottom):
        return jnp.where(bottom > 0.0, top / jnp.where(bottom > 0.0, bottom, 1.0), 0.0)

    norm = over([r * r for r in right])
    curve = over([r * i for r, i in zip(right, images)])
    alpha = ratio(curve, norm)
    spread = over([(i - alpha * r) * (i - alpha * r) for r, i in zip(right, images)])
    lane = lax.broadcasted_iota(jnp.int32, (128, 128), 1)
    out = jnp.zeros((128, 128), F32)
    for i, v in enumerate((norm, curve, spread)):
        tall = jnp.concatenate([v, jnp.zeros((128 - SUM_ROWS, 1), F32)], axis=0)
        out = jnp.where(lane == i, jnp.broadcast_to(tall, out.shape), out)
    stat_own[0] = out.T[:8]

    level8 = lax.broadcasted_iota(jnp.int32, (8, 128), 0)

    def packed(values):
        out = jnp.zeros((8, 128), F32)
        for i, v in enumerate(values):
            out = jnp.where(level8 == i, jnp.broadcast_to(v, out.shape), out)
        return out

    def merged(stats):
        norms, curves, spreads = (stats[:, i : i + 1, :] for i in range(3))
        norm = jnp.sum(norms, axis=0)
        curve = jnp.sum(curves, axis=0)
        shift = ratio(curves, norms) - ratio(curve, norm)[None]
        return norm, curve, jnp.sum(spreads + norms * shift * shift, axis=0)

    stages = ((0, member, mates), (MEMBERS, line, across))

    def stat_copy(stage, i, receiving):
        base, mine, others = stages[stage]
        place, device = others[i]
        slot = base + (place if receiving else mine)
        return remote(
            stat_own.at[stage], stat_got.at[slot], ss_sem.at[base + i], sr_sem.at[slot], device
        )

    for stage, (base, mine, others) in enumerate(stages):
        for i in range(len(others)):
            stat_copy(stage, i, False).start()
        stat_got[base + mine] = stat_own[stage]
        for i in range(len(others)):
            stat_copy(stage, i, True).wait_recv()
        norm, curve, spread = merged(stat_got[pl.ds(base, len(others) + 1)])
        if stage < 1:
            stat_own[stage + 1] = packed((norm, curve, spread))
    step = norm / curve
    scalars = packed((step, step * step * spread / norm))
    sc_out[...] = jnp.concatenate([scalars, jnp.zeros((120, 128), F32)], axis=0).T[:COLS]

    def sent(c):
        c.wait_send()

    for kind in range(len(KINDS)):
        for c in own_copies(kind) + (
            sum((passed_copies(kind, i) for i in range(len(peers))), []) if kind < 2 else []
        ):
            c.wait_send()
    for h in range(2):
        each_row_part(h, range(MEMBERS), sent)
        each_column_part(h, range(MEMBERS), sent)
    for stage, (_, _, others) in enumerate(stages):
        for i in range(len(others)):
            stat_copy(stage, i, False).wait_send()


def on_device(embeddings, weight_in, bias_in, weight_out, lengthscale, noise_level, right_side):
    anywhere = pl.BlockSpec(memory_space=pl.ANY)
    scalar = pl.BlockSpec(memory_space=pltpu.SMEM)
    vmem = pl.BlockSpec(memory_space=pltpu.VMEM)
    dma = pltpu.SemaphoreType.DMA
    images, scalars = pl.pallas_call(
        kernel,
        out_shape=(
            jax.ShapeDtypeStruct((COLS, BLOCK), F32),
            jax.ShapeDtypeStruct((COLS, 128), F32),
        ),
        in_specs=[anywhere, anywhere, anywhere, anywhere, scalar, scalar, anywhere],
        out_specs=[vmem, vmem],
        scratch_shapes=[
            pltpu.VMEM((2, HALF, EMBED), BF16),
            pltpu.VMEM((INNER // NCHUNK, EMBED, NCHUNK), BF16),
            pltpu.VMEM((1, INNER), F32),
            pltpu.VMEM((FEAT, INNER), BF16),
            pltpu.VMEM((COLS, BLOCK), F32),
            pltpu.VMEM((PROBE_ROWS, BLOCK), F32),
            pltpu.VMEM((4, GATHERED, SPAN), BF16),
            pltpu.VMEM((2, SPAN, 256), BF16),
            pltpu.VMEM((4, 256, SPAN), BF16),
            pltpu.VMEM((2, PROBE_ROWS, SPAN), F32),
            pltpu.VMEM((4, PROBE_ROWS, SPAN), F32),
            pltpu.VMEM((2, 2 * MEMBERS, SUM_ROWS, HALF), F32),
            pltpu.VMEM((2, 8, 128), F32),
            pltpu.VMEM((MEMBERS + LINES, 8, 128), F32),
            dma((9,)),
            dma((3, 2 * MEMBERS)),
            dma((3, 2 * MEMBERS)),
            dma((2, 2 * MEMBERS)),
            dma((2, 2 * MEMBERS)),
            dma((MEMBERS + LINES,)),
            dma((MEMBERS + LINES,)),
        ],
        compiler_params=pltpu.CompilerParams(
            collective_id=0, has_side_effects=True, vmem_limit_bytes=56 * 2**20
        ),
        name="cg_step",
    )(
        embeddings, weight_in, bias_in.reshape(1, INNER), weight_out.T, lengthscale, noise_level,
        right_side,
    )
    step_size = scalars[:, 0]
    correction = scalars[:, 1]
    residual = right_side - step_size[:, None] * images
    direction = residual + correction[:, None] * right_side
    return (residual, direction, step_size, correction)


def solution(mesh):
    in_specs = (P(("row", "col"), None), P(), P(), P(), P(), P(), P(None, ("row", "col")))
    out_specs = (P(None, ("row", "col")), P(None, ("row", "col")), P(), P())
    return jax.shard_map(
        on_device, mesh=mesh, in_specs=in_specs, out_specs=out_specs, check_vma=False
    )
```
